32 devices in a mesh: groups: 2 (over y), tp: 4 (over x, core), rep: 4 (over z).
Axes of the slice: x: 2, y: 2, z: 4, core: 2. Of those that a mesh axis runs over, the one named last changes fastest.
Arguments:
- hidden: bfloat16 [768, 8192], P(('groups', 'rep')), parts along dimension 0, may hold values from -6 to 6
- learner_weights: bfloat16 [2, 16384, 4096], P(None, ('groups', 'tp', 'rep')), parts along dimension 1, may hold values from -0.09375 to 0.09375
- slot_cols: int32 [2, 128, 4, 8], P(None, 'groups'), parts along dimension 1, may hold values from 0 to 8, as said below
- cache_keys: bfloat16 [768, 16, 128, 128], P(('groups', 'rep'), 'tp'), parts along dimension 0, may hold values from -700 to 700
- cache_values: bfloat16 [768, 16, 128, 128], P(('groups', 'rep'), 'tp'), parts along dimension 0, may hold values from -6 to 6
- new_keys: bfloat16 [4, 768, 16, 128], P(None, ('groups', 'rep'), 'tp'), parts along dimension 1, may hold values from -6 to 6
- new_values: bfloat16 [4, 768, 16, 128], P(None, ('groups', 'rep'), 'tp'), parts along dimension 1, may hold values from -6 to 6
- cache_len: int32 [768], P(('groups', 'rep')), parts along dimension 0, may hold values from 32 to 128, as said below
Outputs:
- state_out: bfloat16 [768, 8192], P(('groups', 'rep')), parts along dimension 0
The draws below stay inside these ranges and needn't reach their ends.
There are 2 independent parts, one for each index of `groups`. The reference program is written for one: setup_inputs(seed, part) draws one part's arguments, and reference() takes and returns one part's arrays. A program takes and returns all parts, laid end to end along the dimension named above; each array names one. Nothing has to cross between parts.
Inputs may be any that keep to these rules, and one draw needn't show every extreme that they name: `slot_cols`: for each projection, block row i and tp index o, the first entries are the kept local blocks u in rising order and the remaining entries equal 8; how many blocks an index of tp keeps differs widely from index to index. `cache_len`: some row holds exactly 128 cached positions.
All inputs are finite; a program needn't handle non-finite values.
Results may differ from the reference program's by a relative error of at most 0.025.
Values may be sent and summed in bfloat16 or wider, within the bound.
A program may use at most 256 MiB of HBM per device.

```python
import jax
import jax.numpy as jnp
from jax import lax

D = 8192
HD = 128
QH = 32
KVS = 16
STEPS = 4
LEN = 128
ROWS = 384
HF = 4096
HBLK = 32
RBLK = 64
N_TP = 4


def draw_slot_cols(key, part):
    key = jax.random.fold_in(key, 7)
    local_width = HBLK // N_TP
    slot_ids = jnp.arange(local_width, dtype=jnp.int32)
    all_maps = []
    for matrix in range(2):
        level_key, order_key = jax.random.split(jax.random.fold_in(key, matrix))
        levels = jax.random.permutation(level_key, N_TP)
        keep_rows = RBLK * (2 * levels + 1) // (2 * N_TP)
        orders = jax.vmap(lambda sub_key: jax.random.permutation(sub_key, RBLK))(jax.random.split(order_key, HBLK))
        row_ranks = jnp.argsort(orders, axis=1)
        kept_mask = row_ranks < jnp.repeat(keep_rows, local_width)[:, None]
        kept_mask = kept_mask.T.reshape(RBLK, N_TP, local_width)
        ordering = jnp.argsort(jnp.where(kept_mask, 0, local_width) + slot_ids, axis=-1).astype(jnp.int32)
        kept_count = jnp.sum(kept_mask.astype(jnp.int32), axis=-1, keepdims=True)
        all_maps.append(jnp.where(slot_ids < kept_count, ordering, local_width))
    return jnp.stack(all_maps).astype(jnp.int32)


def draw_cache_len(key, part):
    key = jax.random.fold_in(key, 3)
    first_key, second_key = jax.random.split(key)
    lengths = jax.random.randint(first_key, (ROWS,), LEN // 4, LEN + 1)
    longest = jax.random.randint(second_key, (), 0, ROWS)
    return jnp.where(jnp.arange(ROWS) == longest, LEN, lengths).astype(jnp.int32)


def draw_cache_keys(key, part):
    key = jax.random.fold_in(key, 5)
    base_key = jax.random.fold_in(key, 0)
    values = jax.random.normal(base_key, (ROWS, KVS, LEN, HD), jnp.float32)
    return values.astype(jnp.bfloat16)


def shard_levels(own_key, dims, cuts, low, high):
    gain, own = 1.0, jax.random.fold_in(own_key, 6)
    for axis_at, shards_of in cuts:
        heights = jnp.exp(jax.random.uniform(jax.random.fold_in(own, axis_at), (shards_of,), jnp.float32, low / len(cuts), high / len(cuts)))
        gain = gain * jnp.repeat(heights, dims[axis_at] // shards_of).reshape([-1 if axis == axis_at else 1 for axis in range(len(dims))])
    return gain


def centred(key, dims, scale, reach, cuts=(), kind=jnp.bfloat16):
    gain = shard_levels(key, dims, cuts, -0.22, 0.18) if cuts else 1.0
    entries = jax.random.normal(key, dims, jnp.float32) * scale * gain
    return jnp.minimum(jnp.maximum(entries, -reach), reach).astype(kind)


def setup_inputs(seed: int = 0, part: int = 0) -> dict:
    key_of = jax.random.split(jax.random.key(seed), 9)
    part_splits = jax.random.split(jax.random.fold_in(key_of[8], part), 9)
    return {
        "hidden": centred(part_splits[0], (ROWS, D), 1.0, 6.0, ((0, 4),)),
        "learner_weights": centred(part_splits[1], (2, D, HF), (D // 2) ** -0.5, 0.09375, ((1, 16),)),
        "slot_cols": draw_slot_cols(jax.random.fold_in(jax.random.fold_in(key_of[8], part), 71), part),
        "cache_keys": draw_cache_keys(jax.random.fold_in(jax.random.fold_in(key_of[8], part), 71), part),
        "cache_values": centred(part_splits[4], (ROWS, KVS, LEN, HD), 1.0, 6.0, ((0, 4), (1, 4))),
        "new_keys": centred(part_splits[5], (STEPS, ROWS, KVS, HD), 1.0, 6.0, ((1, 4), (2, 4))),
        "new_values": centred(part_splits[6], (STEPS, ROWS, KVS, HD), 1.0, 6.0, ((1, 4), (2, 4))),
        "cache_len": draw_cache_len(jax.random.fold_in(jax.random.fold_in(key_of[8], part), 71), part),
    }


def normalize(state):
    return (state * lax.rsqrt(lax.optimization_barrier(jnp.mean(state * state, axis=-1, keepdims=True)) + 1e-05)).astype(jnp.bfloat16)

def reference(hidden, learner_weights, slot_cols, cache_keys, cache_values, new_keys, new_values, cache_len):
    local_width = HBLK // N_TP
    live_blocks = jnp.any(slot_cols[..., None] == jnp.arange(local_width, dtype=jnp.int32), axis=-2)
    block_mask = live_blocks.reshape(2, RBLK, HBLK)
    block_mask = jnp.repeat(jnp.repeat(block_mask, 128, axis=1), 128, axis=2)
    dense_pair = jnp.where(block_mask, learner_weights, jnp.zeros((), jnp.bfloat16))
    query_weight = dense_pair[0]
    output_weight = dense_pair[1]
    group_size = QH // KVS
    head_part = HF // N_TP
    live_mask = jnp.arange(LEN, dtype=jnp.int32)[None, :] < cache_len[:, None]
    keys_wide = cache_keys.astype(jnp.float32)
    values_wide = cache_values.astype(jnp.float32)
    state = hidden.astype(jnp.float32)
    for step_index in range(STEPS):
        normed = normalize(state)
        queries = (jnp.dot(normed, query_weight, preferred_element_type=jnp.float32) * HD ** (-0.5)).astype(jnp.bfloat16)
        queries = queries.reshape(ROWS, KVS, group_size, HD).astype(jnp.float32)
        cached_scores = jnp.einsum('rvgd,rvld->rvgl', queries, keys_wide)
        cached_scores = jnp.where(live_mask[:, None, None, :], cached_scores, -jnp.inf)
        fresh_keys = new_keys[:step_index + 1].astype(jnp.float32)
        fresh_scores = jnp.einsum('rvgd,trvd->rvgt', queries, fresh_keys)
        largest = jnp.maximum(lax.optimization_barrier(jnp.max(cached_scores, axis=-1)), lax.optimization_barrier(jnp.max(fresh_scores, axis=-1)))
        cached_exp = jnp.exp(cached_scores - largest[..., None])
        fresh_exp = jnp.exp(fresh_scores - largest[..., None])
        denom_sum = lax.optimization_barrier(jnp.sum(cached_exp, axis=-1)) + lax.optimization_barrier(jnp.sum(fresh_exp, axis=-1))
        cached_weights = (cached_exp / denom_sum[..., None]).astype(jnp.bfloat16).astype(jnp.float32)
        fresh_weights = (fresh_exp / denom_sum[..., None]).astype(jnp.bfloat16).astype(jnp.float32)
        attended = jnp.einsum('rvgl,rvld->rvgd', cached_weights, values_wide)
        attended = attended + jnp.einsum('rvgt,trvd->rvgd', fresh_weights, new_values[:step_index + 1].astype(jnp.float32))
        attended = attended.astype(jnp.bfloat16).reshape(ROWS, HF)

        def owner_term(running, owner_index):
            piece = lax.dynamic_slice_in_dim(attended, owner_index * head_part, head_part, 1)
            columns = lax.dynamic_slice_in_dim(output_weight, owner_index * head_part, head_part, 1)
            partial_term = lax.dot_general(piece, columns, (((1,), (1,)), ((), ())), preferred_element_type=jnp.float32)
            rounded = lax.optimization_barrier(partial_term.astype(jnp.bfloat16))
            return (running + rounded.astype(jnp.float32), None)
        update, _ = lax.scan(owner_term, jnp.zeros((ROWS, D), jnp.float32), jnp.arange(N_TP, dtype=jnp.int32))
        state = state + update
    return state.astype(jnp.bfloat16)
```

```python
import functools

import jax
import jax.numpy as jnp
from jax import lax
from jax.experimental import pallas as pl
from jax.experimental.pallas import tpu as pltpu
from jax.sharding import PartitionSpec as P

HD = 128
STEPS = 4
HALVES = 2
PAD = 16
MESH = pl.DeviceIdType.MESH


def kernel(
    dims,
    hid_ref, weights_ref, mask_ref, keys_ref, values_ref, fresh_k_ref, fresh_v_ref, len_ref,
    out_ref,
    xbuf, wbuf, kbuf, vbuf, qsend, qrecv, qs, atts, abuf, usend, urecv, state,
    load_sem, h_send, h_recv, w_send, w_recv, q_send, q_recv, a_send, a_recv,
    u_send, u_recv, x_send, x_recv, o_send, o_recv,
):
    T, R, C, F, half, slots, group, L, width = dims
    heads_dim = F
    rows = R * half
    me_t = lax.axis_index("tp")
    me_r = lax.axis_index("rep")

    def tp_of(d):
        return lax.rem(me_t + d, T)

    def rep_of(d):
        return lax.rem(me_r + d, R)

    loads = [
        pltpu.make_async_copy(keys_ref, kbuf.at[:, :, pl.ds(0, L), :], load_sem.at[0]),
        pltpu.make_async_copy(values_ref, vbuf.at[:, :, pl.ds(0, L), :], load_sem.at[1]),
        pltpu.make_async_copy(fresh_k_ref, kbuf.at[:, :, pl.ds(L, PAD), :], load_sem.at[2]),
        pltpu.make_async_copy(fresh_v_ref, vbuf.at[:, :, pl.ds(L, PAD), :], load_sem.at[3]),
    ]
    columns_own = pl.ds(pl.multiple_of(me_t * F, F), F)
    own_w = [
        pltpu.make_async_copy(weights_ref.at[m, :, columns_own], wbuf.at[m, me_t], load_sem.at[4 + m])
        for m in range(2)
    ]
    own_h = pltpu.make_async_copy(hid_ref.at[me_r], xbuf.at[:, :, me_r], load_sem.at[6])

    barrier = pltpu.get_barrier_semaphore()
    for d in range(1, T):
        pl.semaphore_signal(barrier, inc=1, device_id={"tp": tp_of(d)}, device_id_type=MESH)
    for d in range(1, R):
        pl.semaphore_signal(barrier, inc=1, device_id={"rep": rep_of(d)}, device_id_type=MESH)
    pl.semaphore_wait(barrier, T - 1 + R - 1)

    def w_copy(m, d):
        to = tp_of(d)
        return pltpu.make_async_remote_copy(
            src_ref=weights_ref.at[m, :, pl.ds(pl.multiple_of(to * F, F), F)],
            dst_ref=wbuf.at[m, me_t],
            send_sem=w_send.at[m, d], recv_sem=w_recv.at[m, d],
            device_id={"tp": to}, device_id_type=MESH,
        )

    def h_copy(d):
        to = rep_of(d)
        return pltpu.make_async_remote_copy(
            src_ref=hid_ref.at[to], dst_ref=xbuf.at[:, :, me_r],
            send_sem=h_send.at[d], recv_sem=h_recv.at[d],
            device_id={"rep": to}, device_id_type=MESH,
        )

    def q_copy(b, d):
        to = rep_of(d)
        return pltpu.make_async_remote_copy(
            src_ref=qsend.at[b, to], dst_ref=qrecv.at[b, me_r],
            send_sem=q_send.at[b, d], recv_sem=q_recv.at[b, d],
            device_id={"rep": to}, device_id_type=MESH,
        )

    def a_copy(b, d):
        return pltpu.make_async_remote_copy(
            src_ref=abuf.at[b, me_r], dst_ref=abuf.at[b, me_r],
            send_sem=a_send.at[b, d], recv_sem=a_recv.at[b, d],
            device_id={"rep": rep_of(d)}, device_id_type=MESH,
        )

    def u_copy(b, d):
        to = tp_of(d)
        return pltpu.make_async_remote_copy(
            src_ref=usend.at[b, to], dst_ref=urecv.at[b, me_t],
            send_sem=u_send.at[b, d], recv_sem=u_recv.at[b, d],
            device_id={"tp": to}, device_id_type=MESH,
        )

    def x_copy(b, d):
        return pltpu.make_async_remote_copy(
            src_ref=xbuf.at[b, me_t], dst_ref=xbuf.at[b, me_t],
            send_sem=x_send.at[b, d], recv_sem=x_recv.at[b, d],
            device_id={"tp": tp_of(d)}, device_id_type=MESH,
        )

    def o_copy(b, d):
        to = rep_of(d)
        return pltpu.make_async_remote_copy(
            src_ref=xbuf.at[b, :, to], dst_ref=out_ref.at[me_r, b],
            send_sem=o_send.at[b, d], recv_sem=o_recv.at[b, d],
            device_id={"rep": to}, device_id_type=MESH,
        )

    def mask_weights(m):
        own_w[m].wait()
        for d in range(1, T):
            w_copy(m, d).wait_recv()
        blocks = mask_ref.shape[2]
        side = C // blocks

        @pl.loop(0, T * blocks)
        def _(i):
            t, c = i // blocks, i % blocks
            at = pl.ds(pl.multiple_of(c * side, side), side)
            kept = mask_ref[m, t, c] > 0.5
            block = wbuf[m, t, at, :]
            wbuf[m, t, at, :] = jnp.where(kept, block.astype(jnp.float32), 0.0).astype(jnp.bfloat16)

    tile = min(256, F)

    def q_phase(b):
        @pl.loop(0, F // tile)
        def _(n):
            at = pl.ds(pl.multiple_of(n * tile, tile), tile)
            acc = jnp.zeros((rows, tile), jnp.float32)
            for t in range(T):
                acc += jnp.dot(
                    xbuf[b, t].reshape(rows, C), wbuf[0, t, :, at], preferred_element_type=jnp.float32
                )
            qsend[b, :, :, at] = acc.astype(jnp.bfloat16).reshape(R, half, tile)

        squares = jnp.zeros((rows, 1), jnp.float32)
        for t in range(T):
            x = xbuf[b, t].reshape(rows, C).astype(jnp.float32)
            squares += jnp.sum(x * x, axis=-1, keepdims=True)
        high = squares.astype(jnp.bfloat16).astype(jnp.float32)
        low = squares - high
        lane = lax.broadcasted_iota(jnp.int32, (rows, 128), 1)
        pair = jnp.where(lane < 64, high, low).astype(jnp.bfloat16)
        qsend[b, :, :, pl.ds(F, 128)] = pair.reshape(R, half, 128)
        for d in range(1, R):
            q_copy(b, d).start()
        qrecv[b, me_r] = qsend[b, me_r]

    def a_phase(b, step):
        for d in range(1, R):
            q_copy(b, d).wait_recv()
        squares = jnp.zeros((half, 128), jnp.float32)
        total = jnp.zeros((half, F), jnp.float32)
        for r in range(R):
            squares += qrecv[b, r, :, pl.ds(F, 128)].astype(jnp.float32)
            total += qrecv[b, r, :, pl.ds(0, F)].astype(jnp.float32)
        mean = (squares[:, 0:1] + squares[:, 64:65]) / width
        qs[...] = total * (lax.rsqrt(mean + 1e-05) * HD ** (-0.5))

        @pl.loop(0, half // 8)
        def _(g):
            at = pl.ds(pl.multiple_of(g * 8, 8), 8)
            first = b * half + g * 8
            length = len_ref[pl.ds(pl.multiple_of(first, 8), 8), :]
            length = jnp.concatenate([length] * group, axis=0)
            pos = lax.broadcasted_iota(jnp.int32, (8 * group, L + PAD), 1)
            live = (pos < length) | ((pos >= L) & (pos <= L + step))
            row = lax.rem(lax.broadcasted_iota(jnp.int32, (8 * group, 1), 0), 8)
            for v in range(slots):
                heads = [qs[at, (v * group + k) * HD : (v * group + k + 1) * HD] for k in range(group)]
                query = jnp.concatenate(heads, axis=0).astype(jnp.bfloat16)
                scores = jnp.zeros((8 * group, L + PAD), jnp.float32)
                for i in range(8):
                    one = lax.dot_general(
                        query, kbuf[first + i, v], (((1,), (1,)), ((), ())),
                        preferred_element_type=jnp.float32,
                    )
                    scores = jnp.where(row == i, one, scores)
                scores = jnp.where(live, scores, -jnp.inf)
                top = jnp.max(scores, axis=-1, keepdims=True)
                weights = jnp.exp(scores - top)
                probs = (weights / jnp.sum(weights, axis=-1, keepdims=True)).astype(jnp.bfloat16)
                result = jnp.zeros((8 * group, HD), jnp.float32)
                for i in range(8):
                    one = jnp.dot(probs, vbuf[first + i, v], preferred_element_type=jnp.float32)
                    result = jnp.where(row == i, one, result)
                for k in range(group):
                    atts[at, (v * group + k) * HD : (v * group + k + 1) * HD] = result[k * 8 : (k + 1) * 8]

        abuf[b, me_r] = atts[...].astype(jnp.bfloat16)
        for d in range(1, R):
            a_copy(b, d).start()
        for d in range(1, R):
            q_copy(b, d).wait_send()

    def o_phase(b):
        for d in range(1, R):
            a_copy(b, d).wait_recv()
        for d in range(1, T):
            to = tp_of(d)
            part = lax.dot_general(
                abuf[b].reshape(rows, F), wbuf[1, to], (((1,), (1,)), ((), ())),
                preferred_element_type=jnp.float32,
            )
            usend[b, to] = part.astype(jnp.bfloat16).reshape(R, half, C)
            u_copy(b, d).start()
        part = lax.dot_general(
            abuf[b].reshape(rows, F), wbuf[1, me_t], (((1,), (1,)), ((), ())),
            preferred_element_type=jnp.float32,
        )
        urecv[b, me_t] = part.astype(jnp.bfloat16).reshape(R, half, C)
        for d in range(1, R):
            a_copy(b, d).wait_send()

    def s_phase(b):
        for d in range(1, T):
            u_copy(b, d).wait_recv()
        total = state[b]
        for t in range(T):
            total += urecv[b, t].astype(jnp.float32)
        state[b] = total
        xbuf[b, me_t] = total.astype(jnp.bfloat16)
        for d in range(1, T):
            x_copy(b, d).start()
        for d in range(1, T):
            u_copy(b, d).wait_send()

    def x_wait(b):
        for d in range(1, T):
            x_copy(b, d).wait_recv()
        for d in range(1, T):
            x_copy(b, d).wait_send()

    for d in range(1, T):
        w_copy(0, d).start()
    for d in range(1, R):
        h_copy(d).start()
    own_h.start()
    own_w[0].start()
    for d in range(1, T):
        w_copy(1, d).start()
    own_w[1].start()
    for load in loads:
        load.start()
    own_h.wait()
    for d in range(1, R):
        h_copy(d).wait_recv()
    for b in range(HALVES):
        state[b] = xbuf[b, me_t].astype(jnp.float32)
    mask_weights(0)
    q_phase(0)
    for load in loads:
        load.wait()

    def body(step, carry):
        a_phase(0, step)

        @pl.when(step > 0)
        def _():
            x_wait(1)

        q_phase(1)

        @pl.when(step == 0)
        def _():
            mask_weights(1)

        o_phase(0)
        a_phase(1, step)
        s_phase(0)
        o_phase(1)

        @pl.when(step < STEPS - 1)
        def _():
            x_wait(0)
            q_phase(0)

        s_phase(1)
        return carry

    lax.fori_loop(0, STEPS, body, 0)

    own_o = []
    for b in range(HALVES):
        x_wait(b)
        for d in range(1, R):
            o_copy(b, d).start()
        copy = pltpu.make_async_copy(xbuf.at[b, :, me_r], out_ref.at[me_r, b], load_sem.at[7 + b])
        copy.start()
        own_o.append(copy)
    for b in range(HALVES):
        own_o[b].wait()
        for d in range(1, R):
            o_copy(b, d).wait()
    for d in range(1, R):
        h_copy(d).wait_send()
    for m in range(2):
        for d in range(1, T):
            w_copy(m, d).wait_send()


def on_device(
    hidden, learner_weights, slot_cols, cache_keys, cache_values, new_keys, new_values, cache_len
):
    T = lax.axis_size("tp")
    R = lax.axis_size("rep")
    rows_dev, width = hidden.shape
    C = learner_weights.shape[1]
    F = learner_weights.shape[2] // T
    local_width = slot_cols.shape[3]
    slots, L = cache_keys.shape[1], cache_keys.shape[2]
    group = F // HD // slots
    half = rows_dev // HALVES
    me_t = lax.axis_index("tp")
    me_r = lax.axis_index("rep")

    hid = hidden.reshape(HALVES, half, T, R, C).transpose(3, 0, 2, 1, 4)
    blocks = max(1, C // 128)
    firsts = (jnp.arange(T)[:, None] * R + me_r) * C + jnp.arange(blocks)[None, :] * (C // blocks)
    own_cols = lax.dynamic_index_in_dim(slot_cols, me_t, 2, keepdims=False)
    live = jnp.any(own_cols[..., None] == jnp.arange(local_width, dtype=jnp.int32), axis=-2)
    live = jnp.take(live, firsts.reshape(-1) // 128, axis=1).astype(jnp.float32)
    mask = jnp.repeat(live, 128, axis=-1).reshape(2, T, blocks, 1, F)
    fresh_k = jnp.pad(new_keys.transpose(1, 2, 0, 3), ((0, 0), (0, 0), (0, PAD - STEPS), (0, 0)))
    fresh_v = jnp.pad(new_values.transpose(1, 2, 0, 3), ((0, 0), (0, 0), (0, PAD - STEPS), (0, 0)))
    dims = (T, R, C, F, half, slots, group, L, width)
    bf16, f32 = jnp.bfloat16, jnp.float32
    any_spec = pl.BlockSpec(memory_space=pl.ANY)
    vmem = pl.BlockSpec(memory_space=pltpu.VMEM)
    dma = pltpu.SemaphoreType.DMA
    flops = 2 * rows_dev * R * T * C * F * 2 * STEPS
    out = pl.pallas_call(
        functools.partial(kernel, dims),
        out_shape=jax.ShapeDtypeStruct((R, HALVES, T, half, C), bf16),
        in_specs=[any_spec, any_spec, vmem, any_spec, any_spec, any_spec, any_spec, vmem],
        out_specs=any_spec,
        scratch_shapes=[
            pltpu.VMEM((HALVES, T, R, half, C), bf16),
            pltpu.VMEM((2, T, C, F), bf16),
            pltpu.VMEM((rows_dev, slots, L + PAD, HD), bf16),
            pltpu.VMEM((rows_dev, slots, L + PAD, HD), bf16),
            pltpu.VMEM((HALVES, R, half, F + 128), bf16),
            pltpu.VMEM((HALVES, R, half, F + 128), bf16),
            pltpu.VMEM((half, F), f32),
            pltpu.VMEM((half, F), f32),
            pltpu.VMEM((HALVES, R, half, F), bf16),
            pltpu.VMEM((HALVES, T, R, half, C), bf16),
            pltpu.VMEM((HALVES, T, R, half, C), bf16),
            pltpu.VMEM((HALVES, R, half, C), f32),
            dma((9,)),
            dma((R,)), dma((R,)),
            dma((2, T)), dma((2, T)),
            dma((HALVES, R)), dma((HALVES, R)),
            dma((HALVES, R)), dma((HALVES, R)),
            dma((HALVES, T)), dma((HALVES, T)),
            dma((HALVES, T)), dma((HALVES, T)),
            dma((HALVES, R)), dma((HALVES, R)),
        ],
        compiler_params=pltpu.CompilerParams(
            collective_id=0, has_side_effects=True, vmem_limit_bytes=60 * 1024 * 1024
        ),
        cost_estimate=pl.CostEstimate(flops=flops, bytes_accessed=48 << 20, transcendentals=0),
    )(hid, learner_weights, mask, cache_keys, cache_values, fresh_k, fresh_v, cache_len[:, None])
    return out.transpose(1, 3, 2, 0, 4).reshape(rows_dev, width)


def solution(mesh):
    return jax.shard_map(
        on_device,
        mesh=mesh,
        in_specs=(
            P(("groups", "rep"), None),
            P(None, ("groups", "tp", "rep"), None),
            P(None, "groups", None, None),
            P(("groups", "rep"), "tp", None, None),
            P(("groups", "rep"), "tp", None, None),
            P(None, ("groups", "rep"), "tp", None),
            P(None, ("groups", "rep"), "tp", None),
            P(("groups", "rep")),
        ),
        out_specs=P(("groups", "rep"), None),
        check_vma=False,
    )
```

```python
import functools

import jax
import jax.numpy as jnp
from jax import lax
from jax.experimental import pallas as pl
from jax.experimental.pallas import tpu as pltpu
from jax.sharding import PartitionSpec as P

HD = 128
STEPS = 4
CUTS = 3
PAD = 16
MESH = pl.DeviceIdType.MESH


def kernel(
    dims,
    hid_ref, weights_ref, mask_ref, keys_ref, values_ref, fresh_k_ref, fresh_v_ref, len_ref,
    out_ref,
    xbuf, wbuf, kbuf, vbuf, qsend, qrecv, qs, atts, abuf, usend, urecv, state,
    load_sem, h_send, h_recv, w_send, w_recv, q_send, q_recv, a_send, a_recv,
    u_send, u_recv, x_send, x_recv, o_send, o_recv,
):
    T, R, C, F, cut, slots, group, L, width = dims
    heads_dim = F
    rows = R * cut
    me_t = lax.axis_index("tp")
    me_r = lax.axis_index("rep")

    def tp_of(d):
        return lax.rem(me_t + d, T)

    def rep_of(d):
        return lax.rem(me_r + d, R)

    loads = []
    for j in range(2):
        lanes = pl.ds(j * HD, HD)
        for source, target, at, depth in (
            (keys_ref, kbuf, 0, L), (values_ref, vbuf, 0, L),
            (fresh_k_ref, kbuf, L, PAD), (fresh_v_ref, vbuf, L, PAD),
        ):
            loads.append(
                pltpu.make_async_copy(
                    source.at[:, j], target.at[:, :, pl.ds(at, depth), lanes], load_sem.at[9 + len(loads)]
                )
            )
    columns_own = pl.ds(pl.multiple_of(me_t * F, F), F)
    own_w = [
        pltpu.make_async_copy(weights_ref.at[m, :, columns_own], wbuf.at[m, me_t], load_sem.at[4 + m])
        for m in range(2)
    ]
    own_h = pltpu.make_async_copy(hid_ref.at[me_r], xbuf.at[:, :, me_r], load_sem.at[6])

    barrier = pltpu.get_barrier_semaphore()
    for d in range(1, T):
        pl.semaphore_signal(barrier, inc=1, device_id={"tp": tp_of(d)}, device_id_type=MESH)
    for d in range(1, R):
        pl.semaphore_signal(barrier, inc=1, device_id={"rep": rep_of(d)}, device_id_type=MESH)
    pl.semaphore_wait(barrier, T - 1 + R - 1)

    def w_copy(m, d):
        to = tp_of(d)
        return pltpu.make_async_remote_copy(
            src_ref=weights_ref.at[m, :, pl.ds(pl.multiple_of(to * F, F), F)],
            dst_ref=wbuf.at[m, me_t],
            send_sem=w_send.at[m, d], recv_sem=w_recv.at[m, d],
            device_id={"tp": to}, device_id_type=MESH,
        )

    def h_copy(d):
        to = rep_of(d)
        return pltpu.make_async_remote_copy(
            src_ref=hid_ref.at[to], dst_ref=xbuf.at[:, :, me_r],
            send_sem=h_send.at[d], recv_sem=h_recv.at[d],
            device_id={"rep": to}, device_id_type=MESH,
        )

    def q_copy(b, d):
        to = rep_of(d)
        return pltpu.make_async_remote_copy(
            src_ref=qsend.at[b, to], dst_ref=qrecv.at[b, me_r],
            send_sem=q_send.at[b, d], recv_sem=q_recv.at[b, d],
            device_id={"rep": to}, device_id_type=MESH,
        )

    def a_copy(b, d):
        return pltpu.make_async_remote_copy(
            src_ref=abuf.at[b, me_r], dst_ref=abuf.at[b, me_r],
            send_sem=a_send.at[b, d], recv_sem=a_recv.at[b, d],
            device_id={"rep": rep_of(d)}, device_id_type=MESH,
        )

    def u_copy(b, d):
        to = tp_of(d)
        return pltpu.make_async_remote_copy(
            src_ref=usend.at[b, to], dst_ref=urecv.at[b, me_t],
            send_sem=u_send.at[b, d], recv_sem=u_recv.at[b, d],
            device_id={"tp": to}, device_id_type=MESH,
        )

    def x_copy(b, d):
        return pltpu.make_async_remote_copy(
            src_ref=xbuf.at[b, me_t], dst_ref=xbuf.at[b, me_t],
            send_sem=x_send.at[b, d], recv_sem=x_recv.at[b, d],
            device_id={"tp": tp_of(d)}, device_id_type=MESH,
        )

    def o_copy(b, d):
        to = rep_of(d)
        return pltpu.make_async_remote_copy(
            src_ref=xbuf.at[b, :, to], dst_ref=out_ref.at[me_r, b],
            send_sem=o_send.at[b, d], recv_sem=o_recv.at[b, d],
            device_id={"rep": to}, device_id_type=MESH,
        )

    def mask_weights(m):
        blocks = mask_ref.shape[2]
        side = C // blocks

        @pl.loop(0, T * blocks)
        def _(i):
            t, c = i // blocks, i % blocks
            at = pl.ds(pl.multiple_of(c * side, side), side)
            kept = mask_ref[m, t, c] > 0.5
            block = wbuf[m, t, at, :]
            wbuf[m, t, at, :] = jnp.where(kept, block.astype(jnp.float32), 0.0).astype(jnp.bfloat16)

    tile = min(256, F)

    def q_phase(b):
        @pl.loop(0, F // tile)
        def _(n):
            at = pl.ds(pl.multiple_of(n * tile, tile), tile)
            acc = jnp.zeros((rows, tile), jnp.float32)
            for t in range(T):
                acc += jnp.dot(
                    xbuf[b, t].reshape(rows, C), wbuf[0, t, :, at], preferred_element_type=jnp.float32
                )
            qsend[b, :, :, at] = acc.astype(jnp.bfloat16).reshape(R, cut, tile)

        squares = jnp.zeros((rows, 1), jnp.float32)
        for t in range(T):
            x = xbuf[b, t].reshape(rows, C).astype(jnp.float32)
            squares += jnp.sum(x * x, axis=-1, keepdims=True)
        high = squares.astype(jnp.bfloat16).astype(jnp.float32)
        low = squares - high
        lane = lax.broadcasted_iota(jnp.int32, (rows, 128), 1)
        pair = jnp.where(lane < 64, high, low).astype(jnp.bfloat16)
        qsend[b, :, :, pl.ds(F, 128)] = pair.reshape(R, cut, 128)
        for d in range(1, R):
            q_copy(b, d).start()
        qrecv[b, me_r] = qsend[b, me_r]

    def a_phase(b, step):
        for d in range(1, R):
            q_copy(b, d).wait_recv()
        squares = jnp.zeros((cut, 128), jnp.float32)
        total = jnp.zeros((cut, F), jnp.float32)
        for r in range(R):
            squares += qrecv[b, r, :, pl.ds(F, 128)].astype(jnp.float32)
            total += qrecv[b, r, :, pl.ds(0, F)].astype(jnp.float32)
        mean = (squares[:, 0:1] + squares[:, 64:65]) / width
        qs[...] = total * (lax.rsqrt(mean + 1e-05) * HD ** (-0.5))

        @pl.loop(0, cut // 8)
        def _(g):
            at = pl.ds(pl.multiple_of(g * 8, 8), 8)
            first = b * cut + g * 8
            pair_at = b * (cut // 2) + g * 4
            length = len_ref[pl.ds(pl.multiple_of(first, 8), 8), :]
            length = jnp.concatenate([length] * group, axis=0)
            pos = lax.broadcasted_iota(jnp.int32, (8 * group, L + PAD), 1)
            live = (pos < length) | ((pos >= L) & (pos <= L + step))
            row = lax.rem(lax.broadcasted_iota(jnp.int32, (8 * group, 1), 0), 8)
            for v in range(slots):
                heads = [qs[at, (v * group + k) * HD : (v * group + k + 1) * HD] for k in range(group)]
                query = jnp.concatenate(heads, axis=0)
                scores = jnp.zeros((8 * group, L + PAD), jnp.float32)
                for i in range(4):
                    both = jnp.concatenate(
                        [jnp.where(row == 2 * i + j, query, 0.0) for j in range(2)], axis=1
                    ).astype(jnp.bfloat16)
                    scores += lax.dot_general(
                        both, kbuf[pair_at + i, v], (((1,), (1,)), ((), ())),
                        preferred_element_type=jnp.float32,
                    )
                scores = jnp.where(live, scores, -jnp.inf)
                top = jnp.max(scores, axis=-1, keepdims=True)
                weights = jnp.exp(scores - top)
                probs = (weights / jnp.sum(weights, axis=-1, keepdims=True)).astype(jnp.bfloat16)
                result = jnp.zeros((8 * group, HD), jnp.float32)
                for i in range(4):
                    one = jnp.dot(probs, vbuf[pair_at + i, v], preferred_element_type=jnp.float32)
                    for j in range(2):
                        result = jnp.where(row == 2 * i + j, one[:, j * HD : (j + 1) * HD], result)
                for k in range(group):
                    atts[at, (v * group + k) * HD : (v * group + k + 1) * HD] = result[k * 8 : (k + 1) * 8]

        abuf[b, me_r] = atts[...].astype(jnp.bfloat16)
        for d in range(1, R):
            a_copy(b, d).start()
        for d in range(1, R):
            q_copy(b, d).wait_send()

    def o_phase(b):
        for d in range(1, R):
            a_copy(b, d).wait_recv()
        for d in range(1, T):
            to = tp_of(d)
            part = lax.dot_general(
                abuf[b].reshape(rows, F), wbuf[1, to], (((1,), (1,)), ((), ())),
                preferred_element_type=jnp.float32,
            )
            usend[b, to] = part.astype(jnp.bfloat16).reshape(R, cut, C)
            u_copy(b, d).start()
        part = lax.dot_general(
            abuf[b].reshape(rows, F), wbuf[1, me_t], (((1,), (1,)), ((), ())),
            preferred_element_type=jnp.float32,
        )
        urecv[b, me_t] = part.astype(jnp.bfloat16).reshape(R, cut, C)
        for d in range(1, R):
            a_copy(b, d).wait_send()

    def s_phase(b):
        for d in range(1, T):
            u_copy(b, d).wait_recv()
        total = state[b]
        for t in range(T):
            total += urecv[b, t].astype(jnp.float32)
        state[b] = total
        xbuf[b, me_t] = total.astype(jnp.bfloat16)
        for d in range(1, T):
            x_copy(b, d).start()
        for d in range(1, T):
            u_copy(b, d).wait_send()

    def x_wait(b):
        for d in range(1, T):
            x_copy(b, d).wait_recv()
        for d in range(1, T):
            x_copy(b, d).wait_send()

    own_w[0].start()
    for d in range(1, T):
        w_copy(0, d).start()
    for d in range(1, R):
        h_copy(d).start()
    own_h.start()
    for load in loads:
        load.start()
    own_h.wait()
    for d in range(1, R):
        h_copy(d).wait_recv()
    for b in range(CUTS):
        state[b] = xbuf[b, me_t].astype(jnp.float32)
    own_w[0].wait()
    for d in range(1, T):
        w_copy(0, d).wait_recv()
    own_w[1].start()
    for d in range(1, T):
        w_copy(1, d).start()
    mask_weights(0)
    for load in loads:
        load.wait()

    def body(step, carry):
        later = step > 0
        inside = step < STEPS

        def x_ready(b):
            @pl.when(later & inside)
            def _():
                x_wait(b)

        x_ready(0)

        @pl.when(inside)
        def _():
            q_phase(0)

        @pl.when(later)
        def _():
            s_phase(1)
            o_phase(2)

        @pl.when(inside)
        def _():
            a_phase(0, step)

        x_ready(1)

        @pl.when(inside)
        def _():
            q_phase(1)

        @pl.when(later)
        def _():
            s_phase(2)

        @pl.when(step == 0)
        def _():
            own_w[1].wait()
            for d in range(1, T):
                w_copy(1, d).wait_recv()
            mask_weights(1)

        @pl.when(inside)
        def _():
            o_phase(0)
            a_phase(1, step)

        x_ready(2)

        @pl.when(inside)
        def _():
            q_phase(2)
            s_phase(0)
            o_phase(1)
            a_phase(2, step)

        return carry

    lax.fori_loop(0, STEPS + 1, body, 0)

    own_o = []
    for b in range(CUTS):
        x_wait(b)
        for d in range(1, R):
            o_copy(b, d).start()
        copy = pltpu.make_async_copy(xbuf.at[b, :, me_r], out_ref.at[me_r, b], load_sem.at[17 + b])
        copy.start()
        own_o.append(copy)
    for b in range(CUTS):
        own_o[b].wait()
        for d in range(1, R):
            o_copy(b, d).wait()
    for d in range(1, R):
        h_copy(d).wait_send()
    for m in range(2):
        for d in range(1, T):
            w_copy(m, d).wait_send()


def on_device(
    hidden, learner_weights, slot_cols, cache_keys, cache_values, new_keys, new_values, cache_len
):
    T = lax.axis_size("tp")
    R = lax.axis_size("rep")
    rows_dev, width = hidden.shape
    C = learner_weights.shape[1]
    F = learner_weights.shape[2] // T
    local_width = slot_cols.shape[3]
    slots, L = cache_keys.shape[1], cache_keys.shape[2]
    group = F // HD // slots
    cut = rows_dev // CUTS
    me_t = lax.axis_index("tp")
    me_r = lax.axis_index("rep")

    hid = hidden.reshape(CUTS, cut, T, R, C).transpose(3, 0, 2, 1, 4)
    blocks = max(1, C // 128)
    firsts = (jnp.arange(T)[:, None] * R + me_r) * C + jnp.arange(blocks)[None, :] * (C // blocks)
    own_cols = lax.dynamic_index_in_dim(slot_cols, me_t, 2, keepdims=False)
    live = jnp.any(own_cols[..., None] == jnp.arange(local_width, dtype=jnp.int32), axis=-2)
    live = jnp.take(live, firsts.reshape(-1) // 128, axis=1).astype(jnp.float32)
    mask = jnp.repeat(live, 128, axis=-1).reshape(2, T, blocks, 1, F)
    fresh_k = jnp.pad(new_keys.transpose(1, 2, 0, 3), ((0, 0), (0, 0), (0, PAD - STEPS), (0, 0)))
    fresh_v = jnp.pad(new_values.transpose(1, 2, 0, 3), ((0, 0), (0, 0), (0, PAD - STEPS), (0, 0)))
    dims = (T, R, C, F, cut, slots, group, L, width)
    bf16, f32 = jnp.bfloat16, jnp.float32
    any_spec = pl.BlockSpec(memory_space=pl.ANY)
    vmem = pl.BlockSpec(memory_space=pltpu.VMEM)
    dma = pltpu.SemaphoreType.DMA
    flops = 2 * rows_dev * R * T * C * F * 2 * STEPS
    out = pl.pallas_call(
        functools.partial(kernel, dims),
        out_shape=jax.ShapeDtypeStruct((R, CUTS, T, cut, C), bf16),
        in_specs=[any_spec, any_spec, vmem, any_spec, any_spec, any_spec, any_spec, vmem],
        out_specs=any_spec,
        scratch_shapes=[
            pltpu.VMEM((CUTS, T, R, cut, C), bf16),
            pltpu.VMEM((2, T, C, F), bf16),
            pltpu.VMEM((rows_dev // 2, slots, L + PAD, 2 * HD), bf16),
            pltpu.VMEM((rows_dev // 2, slots, L + PAD, 2 * HD), bf16),
            pltpu.VMEM((CUTS, R, cut, F + 128), bf16),
            pltpu.VMEM((CUTS, R, cut, F + 128), bf16),
            pltpu.VMEM((cut, F), f32),
            pltpu.VMEM((cut, F), f32),
            pltpu.VMEM((CUTS, R, cut, F), bf16),
            pltpu.VMEM((CUTS, T, R, cut, C), bf16),
            pltpu.VMEM((CUTS, T, R, cut, C), bf16),
            pltpu.VMEM((CUTS, R, cut, C), f32),
            dma((9 + 8 + CUTS,)),
            dma((R,)), dma((R,)),
            dma((2, T)), dma((2, T)),
            dma((CUTS, R)), dma((CUTS, R)),
            dma((CUTS, R)), dma((CUTS, R)),
            dma((CUTS, T)), dma((CUTS, T)),
            dma((CUTS, T)), dma((CUTS, T)),
            dma((CUTS, R)), dma((CUTS, R)),
        ],
        compiler_params=pltpu.CompilerParams(
            collective_id=0, has_side_effects=True, vmem_limit_bytes=60 * 1024 * 1024
        ),
        cost_estimate=pl.CostEstimate(flops=flops, bytes_accessed=48 << 20, transcendentals=0),
    )(hid, learner_weights, mask, *(a.reshape(rows_dev // 2, 2, *a.shape[1:]) for a in (cache_keys, cache_values, fresh_k, fresh_v)), cache_len[:, None])
    return out.transpose(1, 3, 2, 0, 4).reshape(rows_dev, width)


def solution(mesh):
    return jax.shard_map(
        on_device,
        mesh=mesh,
        in_specs=(
            P(("groups", "rep"), None),
            P(None, ("groups", "tp", "rep"), None),
            P(None, "groups", None, None),
            P(("groups", "rep"), "tp", None, None),
            P(("groups", "rep"), "tp", None, None),
            P(None, ("groups", "rep"), "tp", None),
            P(None, ("groups", "rep"), "tp", None),
            P(("groups", "rep")),
        ),
        out_specs=P(("groups", "rep"), None),
        check_vma=False,
    )
```

```python
import functools

import jax
import jax.numpy as jnp
from jax import lax
from jax.experimental import pallas as pl
from jax.experimental.pallas import tpu as pltpu
from jax.sharding import PartitionSpec as P

HD = 128
STEPS = 4
CUTS = 3
PAD = 16
MESH = pl.DeviceIdType.MESH


def kernel(
    dims,
    hid_ref, weights_ref, mask_ref, keys_ref, values_ref, fresh_k_ref, fresh_v_ref, len_ref,
    out_ref,
    xbuf, wbuf, kbuf, vbuf, qsend, qrecv, qs, atts, abuf, usend, urecv, state,
    load_sem, h_send, h_recv, w_send, w_recv, q_send, q_recv, a_send, a_recv,
    u_send, u_recv, x_send, x_recv, o_send, o_recv,
    hs_send, hs_recv, os_send, os_recv,
):
    T, R, C, F, cut, slots, group, L, width = dims
    heads_dim = F
    rows = R * cut
    me_t = lax.axis_index("tp")
    me_r = lax.axis_index("rep")
    core = lax.rem(me_t, 2)
    sibling = me_t + 1 - 2 * core

    def tp_of(d):
        return lax.rem(me_t + d, T)

    def rep_of(d):
        return lax.rem(me_r + d, R)

    loads = []
    for j in range(2):
        lanes = pl.ds(j * HD, HD)
        for source, target, at, depth in (
            (keys_ref, kbuf, 0, L), (values_ref, vbuf, 0, L),
            (fresh_k_ref, kbuf, L, PAD), (fresh_v_ref, vbuf, L, PAD),
        ):
            loads.append(
                pltpu.make_async_copy(
                    source.at[:, j], target.at[:, :, pl.ds(at, depth), lanes], load_sem.at[9 + len(loads)]
                )
            )
    columns_own = pl.ds(pl.multiple_of(me_t * F, F), F)
    own_w = [
        pltpu.make_async_copy(weights_ref.at[m, :, columns_own], wbuf.at[m, me_t], load_sem.at[4 + m])
        for m in range(2)
    ]
    own_h = pltpu.make_async_copy(hid_ref.at[me_r], xbuf.at[:, :, :, me_r], load_sem.at[6])

    barrier = pltpu.get_barrier_semaphore()
    for d in range(1, T):
        pl.semaphore_signal(barrier, inc=1, device_id={"tp": tp_of(d)}, device_id_type=MESH)
    for d in range(1, R):
        pl.semaphore_signal(barrier, inc=1, device_id={"rep": rep_of(d)}, device_id_type=MESH)
    pl.semaphore_wait(barrier, T - 1 + R - 1)

    def w_copy(m, d):
        to = tp_of(d)
        return pltpu.make_async_remote_copy(
            src_ref=weights_ref.at[m, :, pl.ds(pl.multiple_of(to * F, F), F)],
            dst_ref=wbuf.at[m, me_t],
            send_sem=w_send.at[m, d], recv_sem=w_recv.at[m, d],
            device_id={"tp": to}, device_id_type=MESH,
        )

    def h_copy(d):
        to = rep_of(d)
        return pltpu.make_async_remote_copy(
            src_ref=hid_ref.at[to, :, :, core], dst_ref=xbuf.at[:, :, core, me_r],
            send_sem=h_send.at[d], recv_sem=h_recv.at[d],
            device_id={"rep": to}, device_id_type=MESH,
        )

    def h_share(d):
        at = rep_of(d)
        return pltpu.make_async_remote_copy(
            src_ref=xbuf.at[:, :, core, at], dst_ref=xbuf.at[:, :, core, at],
            send_sem=hs_send.at[d], recv_sem=hs_recv.at[d],
            device_id={"tp": sibling}, device_id_type=MESH,
        )

    def q_copy(b, d):
        to = rep_of(d)
        return pltpu.make_async_remote_copy(
            src_ref=qsend.at[b, to], dst_ref=qrecv.at[b, me_r],
            send_sem=q_send.at[b, d], recv_sem=q_recv.at[b, d],
            device_id={"rep": to}, device_id_type=MESH,
        )

    def a_copy(b, d):
        return pltpu.make_async_remote_copy(
            src_ref=abuf.at[b, me_r], dst_ref=abuf.at[b, me_r],
            send_sem=a_send.at[b, d], recv_sem=a_recv.at[b, d],
            device_id={"rep": rep_of(d)}, device_id_type=MESH,
        )

    def u_copy(b, d):
        to = tp_of(d)
        return pltpu.make_async_remote_copy(
            src_ref=usend.at[b, to], dst_ref=urecv.at[b, me_t],
            send_sem=u_send.at[b, d], recv_sem=u_recv.at[b, d],
            device_id={"tp": to}, device_id_type=MESH,
        )

    def x_copy(b, d):
        return pltpu.make_async_remote_copy(
            src_ref=xbuf.at[b, me_t // 2, core], dst_ref=xbuf.at[b, me_t // 2, core],
            send_sem=x_send.at[b, d], recv_sem=x_recv.at[b, d],
            device_id={"tp": tp_of(d)}, device_id_type=MESH,
        )

    def o_copy(b, d):
        to = rep_of(d)
        return pltpu.make_async_remote_copy(
            src_ref=xbuf.at[b, :, core, to], dst_ref=out_ref.at[me_r, b, :, core],
            send_sem=o_send.at[b, d], recv_sem=o_recv.at[b, d],
            device_id={"rep": to}, device_id_type=MESH,
        )

    def o_share(b, d):
        at = lax.rem(me_r + R - d, R)
        return pltpu.make_async_remote_copy(
            src_ref=out_ref.at[at, b, :, core], dst_ref=out_ref.at[at, b, :, core],
            send_sem=os_send.at[b, d], recv_sem=os_recv.at[b, d],
            device_id={"tp": sibling}, device_id_type=MESH,
        )

    def mask_weights(m):
        blocks = mask_ref.shape[2]
        side = C // blocks

        @pl.loop(0, T * blocks)
        def _(i):
            t, c = i // blocks, i % blocks
            at = pl.ds(pl.multiple_of(c * side, side), side)
            kept = mask_ref[m, t, c] > 0.5
            block = wbuf[m, t, at, :]
            wbuf[m, t, at, :] = jnp.where(kept, block.astype(jnp.float32), 0.0).astype(jnp.bfloat16)

    tile = min(256, F)

    def q_phase(b):
        @pl.loop(0, F // tile)
        def _(n):
            at = pl.ds(pl.multiple_of(n * tile, tile), tile)
            acc = jnp.zeros((rows, tile), jnp.float32)
            for t in range(T):
                acc += jnp.dot(
                    xbuf[b, t // 2, t % 2].reshape(rows, C), wbuf[0, t, :, at], preferred_element_type=jnp.float32
                )
            qsend[b, :, :, at] = acc.astype(jnp.bfloat16).reshape(R, cut, tile)

        squares = jnp.zeros((rows, 1), jnp.float32)
        for t in range(T):
            x = xbuf[b, t // 2, t % 2].reshape(rows, C).astype(jnp.float32)
            squares += jnp.sum(x * x, axis=-1, keepdims=True)
        high = squares.astype(jnp.bfloat16).astype(jnp.float32)
        low = squares - high
        lane = lax.broadcasted_iota(jnp.int32, (rows, 128), 1)
        pair = jnp.where(lane < 64, high, low).astype(jnp.bfloat16)
        qsend[b, :, :, pl.ds(F, 128)] = pair.reshape(R, cut, 128)
        for d in range(1, R):
            q_copy(b, d).start()
        qrecv[b, me_r] = qsend[b, me_r]

    def a_phase(b, step):
        for d in range(1, R):
            q_copy(b, d).wait_recv()
        squares = jnp.zeros((cut, 128), jnp.float32)
        total = jnp.zeros((cut, F), jnp.float32)
        for r in range(R):
            squares += qrecv[b, r, :, pl.ds(F, 128)].astype(jnp.float32)
            total += qrecv[b, r, :, pl.ds(0, F)].astype(jnp.float32)
        mean = (squares[:, 0:1] + squares[:, 64:65]) / width
        qs[...] = total * (lax.rsqrt(mean + 1e-05) * HD ** (-0.5))

        @pl.loop(0, cut // 8)
        def _(g):
            at = pl.ds(pl.multiple_of(g * 8, 8), 8)
            first = b * cut + g * 8
            pair_at = b * (cut // 2) + g * 4
            length = len_ref[pl.ds(pl.multiple_of(first, 8), 8), :]
            length = jnp.concatenate([length] * group, axis=0)
            pos = lax.broadcasted_iota(jnp.int32, (8 * group, L + PAD), 1)
            live = (pos < length) | ((pos >= L) & (pos <= L + step))
            row = lax.rem(lax.broadcasted_iota(jnp.int32, (8 * group, 1), 0), 8)
            parts = []
            for v in range(slots):
                heads = [qs[at, (v * group + k) * HD : (v * group + k + 1) * HD] for k in range(group)]
                query = jnp.concatenate(heads, axis=0)
                part = jnp.zeros((8 * group, L + PAD), jnp.float32)
                for i in range(4):
                    both = jnp.concatenate(
                        [jnp.where(row == 2 * i + j, query, 0.0) for j in range(2)], axis=1
                    ).astype(jnp.bfloat16)
                    part += lax.dot_general(
                        both, kbuf[pair_at + i, v], (((1,), (1,)), ((), ())),
                        preferred_element_type=jnp.float32,
                    )
                parts.append(jnp.where(live, part, -jnp.inf))
            scores = jnp.concatenate(parts, axis=0)
            weights = jnp.exp(scores - jnp.max(scores, axis=-1, keepdims=True))
            probs = (weights / jnp.sum(weights, axis=-1, keepdims=True)).astype(jnp.bfloat16)
            found = [
                [
                    jnp.dot(
                        probs[v * 8 * group : (v + 1) * 8 * group], vbuf[pair_at + i, v],
                        preferred_element_type=jnp.float32,
                    )
                    for i in range(4)
                ]
                for v in range(slots)
            ]
            for v in range(slots):
                result = jnp.zeros((8 * group, HD), jnp.float32)
                for i in range(4):
                    for j in range(2):
                        result = jnp.where(row == 2 * i + j, found[v][i][:, j * HD : (j + 1) * HD], result)
                for k in range(group):
                    atts[at, (v * group + k) * HD : (v * group + k + 1) * HD] = result[k * 8 : (k + 1) * 8]

        abuf[b, me_r] = atts[...].astype(jnp.bfloat16)
        for d in range(1, R):
            a_copy(b, d).start()
        for d in range(1, R):
            q_copy(b, d).wait_send()

    def o_phase(b):
        for d in range(1, R):
            a_copy(b, d).wait_recv()
        for d in range(1, T):
            to = tp_of(d)
            part = lax.dot_general(
                abuf[b].reshape(rows, F), wbuf[1, to], (((1,), (1,)), ((), ())),
                preferred_element_type=jnp.float32,
            )
            usend[b, to] = part.astype(jnp.bfloat16).reshape(R, cut, C)
            u_copy(b, d).start()
        part = lax.dot_general(
            abuf[b].reshape(rows, F), wbuf[1, me_t], (((1,), (1,)), ((), ())),
            preferred_element_type=jnp.float32,
        )
        urecv[b, me_t] = part.astype(jnp.bfloat16).reshape(R, cut, C)
        for d in range(1, R):
            a_copy(b, d).wait_send()

    def s_phase(b):
        for d in range(1, T):
            u_copy(b, d).wait_recv()
        total = state[b]
        for t in range(T):
            total += urecv[b, t].astype(jnp.float32)
        state[b] = total
        xbuf[b, me_t // 2, core] = total.astype(jnp.bfloat16)
        for d in range(1, T):
            x_copy(b, d).start()
        for d in range(1, T):
            u_copy(b, d).wait_send()

    def x_wait(b):
        for d in range(1, T):
            x_copy(b, d).wait_recv()
        for d in range(1, T):
            x_copy(b, d).wait_send()

    own_w[0].start()
    for d in range(1, T):
        w_copy(0, d).start()
    for d in range(1, R):
        h_copy(d).start()
    own_h.start()
    for load in loads:
        load.start()
    own_h.wait()
    for d in range(1, R):
        h_copy(R - d).wait_recv()
        h_share(d).start()
    for d in range(1, R):
        h_share(d).wait_recv()
    for b in range(CUTS):
        state[b] = xbuf[b, me_t // 2, core].astype(jnp.float32)
    own_w[0].wait()
    for d in range(1, T):
        w_copy(0, d).wait_recv()
    own_w[1].start()
    for d in range(1, T):
        w_copy(1, d).start()
    mask_weights(0)
    for load in loads:
        load.wait()
    for d in range(1, R):
        h_share(d).wait_send()

    def body(step, carry):
        later = step > 0
        inside = step < STEPS

        def x_ready(b):
            @pl.when(later & inside)
            def _():
                x_wait(b)

        x_ready(0)

        @pl.when(inside)
        def _():
            q_phase(0)

        @pl.when(later)
        def _():
            s_phase(1)
            o_phase(2)

        @pl.when(inside)
        def _():
            a_phase(0, step)

        x_ready(1)

        @pl.when(inside)
        def _():
            q_phase(1)

        @pl.when(later)
        def _():
            s_phase(2)

        @pl.when(step == 0)
        def _():
            own_w[1].wait()
            for d in range(1, T):
                w_copy(1, d).wait_recv()
            mask_weights(1)

        @pl.when(inside)
        def _():
            o_phase(0)
            a_phase(1, step)

        x_ready(2)

        @pl.when(inside)
        def _():
            q_phase(2)
            s_phase(0)
            o_phase(1)
            a_phase(2, step)

        return carry

    lax.fori_loop(0, STEPS + 1, body, 0)

    own_o = []
    for b in range(CUTS):
        x_wait(b)
        for d in range(1, R):
            o_copy(b, d).start()
        copy = pltpu.make_async_copy(xbuf.at[b, :, :, me_r], out_ref.at[me_r, b], load_sem.at[17 + b])
        copy.start()
        own_o.append(copy)
    for b in range(CUTS):
        own_o[b].wait()
        for d in range(1, R):
            o_copy(b, d).wait()
            o_share(b, d).start()
    for b in range(CUTS):
        for d in range(1, R):
            o_share(b, d).wait()
    for d in range(1, R):
        h_copy(d).wait_send()
    for m in range(2):
        for d in range(1, T):
            w_copy(m, d).wait_send()


def on_device(
    hidden, learner_weights, slot_cols, cache_keys, cache_values, new_keys, new_values, cache_len
):
    T = lax.axis_size("tp")
    R = lax.axis_size("rep")
    rows_dev, width = hidden.shape
    C = learner_weights.shape[1]
    F = learner_weights.shape[2] // T
    local_width = slot_cols.shape[3]
    slots, L = cache_keys.shape[1], cache_keys.shape[2]
    group = F // HD // slots
    cut = rows_dev // CUTS
    me_t = lax.axis_index("tp")
    me_r = lax.axis_index("rep")

    hid = hidden.reshape(CUTS, cut, T // 2, 2, R, C).transpose(4, 0, 2, 3, 1, 5)
    blocks = max(1, C // 128)
    firsts = (jnp.arange(T)[:, None] * R + me_r) * C + jnp.arange(blocks)[None, :] * (C // blocks)
    own_cols = lax.dynamic_index_in_dim(slot_cols, me_t, 2, keepdims=False)
    live = jnp.any(own_cols[..., None] == jnp.arange(local_width, dtype=jnp.int32), axis=-2)
    live = jnp.take(live, firsts.reshape(-1) // 128, axis=1).astype(jnp.float32)
    mask = jnp.repeat(live, 128, axis=-1).reshape(2, T, blocks, 1, F)
    fresh_k = jnp.pad(new_keys.transpose(1, 2, 0, 3), ((0, 0), (0, 0), (0, PAD - STEPS), (0, 0)))
    fresh_v = jnp.pad(new_values.transpose(1, 2, 0, 3), ((0, 0), (0, 0), (0, PAD - STEPS), (0, 0)))
    dims = (T, R, C, F, cut, slots, group, L, width)
    bf16, f32 = jnp.bfloat16, jnp.float32
    any_spec = pl.BlockSpec(memory_space=pl.ANY)
    vmem = pl.BlockSpec(memory_space=pltpu.VMEM)
    dma = pltpu.SemaphoreType.DMA
    flops = 2 * rows_dev * R * T * C * F * 2 * STEPS
    out = pl.pallas_call(
        functools.partial(kernel, dims),
        out_shape=jax.ShapeDtypeStruct((R, CUTS, T // 2, 2, cut, C), bf16),
        in_specs=[any_spec, any_spec, vmem, any_spec, any_spec, any_spec, any_spec, vmem],
        out_specs=any_spec,
        scratch_shapes=[
            pltpu.VMEM((CUTS, T // 2, 2, R, cut, C), bf16),
            pltpu.VMEM((2, T, C, F), bf16),
            pltpu.VMEM((rows_dev // 2, slots, L + PAD, 2 * HD), bf16),
            pltpu.VMEM((rows_dev // 2, slots, L + PAD, 2 * HD), bf16),
            pltpu.VMEM((CUTS, R, cut, F + 128), bf16),
            pltpu.VMEM((CUTS, R, cut, F + 128), bf16),
            pltpu.VMEM((cut, F), f32),
            pltpu.VMEM((cut, F), f32),
            pltpu.VMEM((CUTS, R, cut, F), bf16),
            pltpu.VMEM((CUTS, T, R, cut, C), bf16),
            pltpu.VMEM((CUTS, T, R, cut, C), bf16),
            pltpu.VMEM((CUTS, R, cut, C), f32),
            dma((9 + 8 + CUTS,)),
            dma((R,)), dma((R,)),
            dma((2, T)), dma((2, T)),
            dma((CUTS, R)), dma((CUTS, R)),
            dma((CUTS, R)), dma((CUTS, R)),
            dma((CUTS, T)), dma((CUTS, T)),
            dma((CUTS, T)), dma((CUTS, T)),
            dma((CUTS, R)), dma((CUTS, R)),
            dma((R,)), dma((R,)), dma((CUTS, R)), dma((CUTS, R)),
        ],
        compiler_params=pltpu.CompilerParams(
            collective_id=0, has_side_effects=True, vmem_limit_bytes=60 * 1024 * 1024
        ),
        cost_estimate=pl.CostEstimate(flops=flops, bytes_accessed=48 << 20, transcendentals=0),
    )(hid, learner_weights, mask, *(a.reshape(rows_dev // 2, 2, *a.shape[1:]) for a in (cache_keys, cache_values, fresh_k, fresh_v)), cache_len[:, None])
    return out.transpose(1, 4, 2, 3, 0, 5).reshape(rows_dev, width)


def solution(mesh):
    return jax.shard_map(
        on_device,
        mesh=mesh,
        in_specs=(
            P(("groups", "rep"), None),
            P(None, ("groups", "tp", "rep"), None),
            P(None, "groups", None, None),
            P(("groups", "rep"), "tp", None, None),
            P(("groups", "rep"), "tp", None, None),
            P(None, ("groups", "rep"), "tp", None),
            P(None, ("groups", "rep"), "tp", None),
            P(("groups", "rep")),
        ),
        out_specs=P(("groups", "rep"), None),
        check_vma=False,
    )
```
